1024 devices in a mesh: dp: 16 (over z, core), expert: 64 (over x, y).
Axes of the slice: x: 8, y: 8, z: 8, core: 2. Of those that a mesh axis runs over, the one named last changes fastest.
Arguments:
- expert_inputs: bfloat16 [16, 64, 240, 2048], P('dp', 'expert'), may hold values from -6 to 6
- up_cotangent: bfloat16 [16, 64, 240, 768], P('dp', 'expert'), may hold values from -0.375 to 0.375
- row_counts: int32 [16, 64], P('dp', 'expert'), may hold values from 60 to 240, as said below
- weights: bfloat16 [2048, 64, 768], P('dp', 'expert'), may hold values from -6 to 6
- first_moment: bfloat16 [2048, 64, 768], P('dp', 'expert'), may hold values from -6 to 6
- second_moment: bfloat16 [2048, 64, 768], P('dp', 'expert'), may hold values from 0.049804688 to 2
- old_expert: int32 [64], replicated, may hold values from 0 to 63, each once
- new_expert: int32 [128], replicated, may hold values from 0 to 63, as said below
- slot_counts: int32 [64], replicated, may hold values from 1 to 2, as said below
Outputs:
- new_weights: bfloat16 [2048, 128, 768], P('dp', 'expert')
- new_first: bfloat16 [2048, 128, 768], P('dp', 'expert')
- new_second: bfloat16 [2048, 128, 768], P('dp', 'expert')
The draws below stay inside these ranges and needn't reach their ends.
Inputs may be any that keep to these rules, and one draw needn't show every extreme that they name: `row_counts`: some replica of some expert has exactly 240 rows in every draw. `new_expert`: every expert is named by at least one live new slot; the live slots of one device name different experts; entries of slots that are not live are arbitrary expert numbers. `slot_counts`: every device keeps at least one expert; in every draw some device has 2 live slots and some other device one.
All inputs are finite; a program needn't handle non-finite values.
Results may differ from the reference program's by a relative error of at most 0.012.
Values may be sent and summed in bfloat16 or wider, within the bound.
A program may use at most 32 MiB of HBM per device.

```python
import math
import jax
import jax.numpy as jnp
from jax import lax

D = 2048
FF = 768
ROWS = 240
SLOTS = 2
EXPERTS = 64
NEW_SLOTS = 128
TOKENS_EXPERT = 3840
N_DP = 16


def placement_tables(key):
    first_key, count_key, pick_key, extra_key = jax.random.split(key, 4)
    first = jax.random.permutation(first_key, EXPERTS).astype(jnp.int32)
    counts = jax.random.randint(count_key, (EXPERTS,), 1, SLOTS + 1, dtype=jnp.int32)
    chosen = jax.random.randint(pick_key, (2,), 0, EXPERTS, dtype=jnp.int32)
    full_device = chosen[0]
    single_device = (full_device + 1 + chosen[1] % (EXPERTS - 1)) % EXPERTS
    counts = counts.at[full_device].set(SLOTS).at[single_device].set(1)
    offsets = jax.random.randint(extra_key, (EXPERTS, SLOTS - 1), 1, EXPERTS, dtype=jnp.int32)
    extra = (first[:, None] + offsets) % EXPERTS
    table = jnp.concatenate([first[:, None], extra], axis=1).reshape(EXPERTS * SLOTS)
    return (table.astype(jnp.int32), counts.astype(jnp.int32))


def draw_new_expert(key, part):
    table, counts = placement_tables(key)
    return table


def draw_slot_counts(key, part):
    table, counts = placement_tables(key)
    return counts


def draw_row_counts(key, part):
    key = jax.random.fold_in(key, 5)
    count_key, place_key = jax.random.split(key, 2)
    counts = jax.random.randint(count_key, (N_DP * EXPERTS,), ROWS // 4, ROWS + 1, dtype=jnp.int32)
    position = jax.random.randint(place_key, (), 0, N_DP * EXPERTS, dtype=jnp.int32)
    counts = counts.at[position].set(ROWS)
    return counts.reshape(N_DP, EXPERTS)


def block_levels(key, shape, cuts, low, high):
    gain = 1.0
    for dim, blocks in cuts:
        heights = jax.random.uniform(jax.random.fold_in(jax.random.fold_in(key, 6), dim), (blocks,), jnp.float32, low / len(cuts), high / len(cuts))
        gain = gain * jnp.repeat(jnp.exp(heights), shape[dim] // blocks).reshape((-1,) + (1,) * (len(shape) - 1 - dim))
    return gain


def noise(rng, shape, width, most, pieces=(), held_as=jnp.bfloat16):
    level = block_levels(rng, shape, pieces, -0.22, 0.18) if pieces else 1.0
    array = jax.random.normal(rng, shape, jnp.float32) * width * level
    return jnp.minimum(jnp.maximum(array, -most), most).astype(held_as)


def setup_inputs(seed: int = 0) -> dict:
    seeds = jax.random.split(jax.random.key(seed), 10)
    expert_inputs = noise(seeds[0], (N_DP, EXPERTS, ROWS, D), 1.0, 6.0, ((0, 16), (1, 64)))
    up_cotangent = noise(seeds[1], (N_DP, EXPERTS, ROWS, FF), (1.5 / TOKENS_EXPERT ** 0.5), 0.375, ((0, 16), (1, 64)))
    row_counts = draw_row_counts(jax.random.fold_in(seeds[9], 71), 0)
    weights = noise(seeds[3], (D, EXPERTS, FF), 0.5, 6.0, ((0, 16), (1, 64)))
    first_moment = noise(seeds[4], (D, EXPERTS, FF), 0.4, 6.0, ((0, 16), (1, 64)))
    second_moment = jnp.clip(jnp.exp(math.log(2.0) - 3.6927934 * jax.random.uniform(seeds[5], (D, EXPERTS, FF), jnp.float32) ** block_levels(seeds[5], (D, EXPERTS, FF), ((0, 16), (1, 64)), -0.2, 0.2)), 0.049804688, 2.0).astype(jnp.bfloat16)
    old_expert = jax.random.permutation(seeds[6], EXPERTS).astype(jnp.int32)
    new_expert = draw_new_expert(jax.random.fold_in(seeds[9], 71), 0)
    slot_counts = draw_slot_counts(jax.random.fold_in(seeds[9], 71), 0)
    return dict(expert_inputs=expert_inputs, up_cotangent=up_cotangent, row_counts=row_counts, weights=weights, first_moment=first_moment, second_moment=second_moment, old_expert=old_expert, new_expert=new_expert, slot_counts=slot_counts)


beta_one = 0.9
beta_two = 0.95
learn_rate = 0.05
decay_rate = 0.1
epsilon = 1e-08
correct_one = 0.9999734386011124
correct_two = 0.994079470779666

def adamw_step(gradient, weight, first, second):
    first_new = beta_one * first.astype(jnp.float32) + (1.0 - beta_one) * gradient
    second_new = beta_two * second.astype(jnp.float32) + (1.0 - beta_two) * gradient * gradient
    direction = first_new / correct_one / (jnp.sqrt(second_new / correct_two) + epsilon)
    weight_full = weight.astype(jnp.float32)
    weight_new = weight_full - learn_rate * (direction + decay_rate * weight_full)
    return (weight_new.astype(jnp.bfloat16), first_new.astype(jnp.bfloat16), second_new.astype(jnp.bfloat16))

def reference(expert_inputs, up_cotangent, row_counts, weights, first_moment, second_moment, old_expert, new_expert, slot_counts):
    positions = jnp.arange(ROWS, dtype=jnp.int32)

    def per_expert(index):
        inputs = expert_inputs[:, index]
        cotangent = up_cotangent[:, index]
        live_rows = positions[None, :] < row_counts[:, index][:, None]
        masked = jnp.where(live_rows[:, :, None], cotangent, jnp.zeros_like(cotangent))
        product = jnp.einsum('prd,prf->pdf', inputs.astype(jnp.float32), masked.astype(jnp.float32))
        rounded = lax.optimization_barrier(product.astype(jnp.bfloat16))
        gradient = lax.optimization_barrier(jnp.sum(rounded.astype(jnp.float32), axis=0))
        return adamw_step(gradient, weights[:, index], first_moment[:, index], second_moment[:, index])
    updated_w, updated_m, updated_v = lax.map(per_expert, jnp.arange(EXPERTS, dtype=jnp.int32))
    matches = old_expert[None, :] == new_expert[:, None]
    source = lax.optimization_barrier(jnp.sum(jnp.where(matches, jnp.arange(EXPERTS, dtype=jnp.int32)[None, :], 0), axis=1)).astype(jnp.int32)
    slot_index = jnp.arange(NEW_SLOTS, dtype=jnp.int32)
    keep_slot = slot_index % SLOTS < jnp.repeat(slot_counts, SLOTS, total_repeat_length=NEW_SLOTS)

    def place(table):
        chosen = jnp.take(table, source, axis=0)
        chosen = jnp.where(keep_slot[:, None, None], chosen, jnp.zeros_like(chosen))
        return jnp.transpose(chosen, (1, 0, 2))
    return (place(updated_w), place(updated_m), place(updated_v))
```

```python
import functools
import math

import jax
import jax.numpy as jnp
from jax import lax
from jax.experimental import pallas as pl
from jax.experimental.pallas import tpu as pltpu
from jax.sharding import PartitionSpec as P

MESH = pl.DeviceIdType.MESH
f32, bf16 = jnp.float32, jnp.bfloat16

beta_one = 0.9
beta_two = 0.95
learn_rate = 0.05
decay_rate = 0.1
epsilon = 1e-08
correct_one = 0.9999734386011124
correct_two = 0.994079470779666


def adamw_step(gradient, weight, first, second):
    first_new = beta_one * first + (1.0 - beta_one) * gradient
    second_new = beta_two * second + (1.0 - beta_two) * gradient * gradient
    direction = first_new / correct_one / (jnp.sqrt(second_new / correct_two) + epsilon)
    weight_new = weight - learn_rate * (direction + decay_rate * weight)
    return weight_new, first_new, second_new


def kernel(
    n_z, n_x, n_y, halves,
    count_ref, table_ref, inputs_ref, cotangent_ref, weights_ref, first_ref, second_ref,
    out_ref,
    masked, masked_other, inputs_other, away, toward, state, state_all, grad, grad_all, updated, chosen,
    pair_send, pair_recv, away_send, away_recv, toward_send, toward_recv,
    state_send, state_recv, grad_send, grad_recv, out_send, out_recv, own_sem,
):
    dp, me = lax.axis_index("dp"), lax.axis_index("expert")
    z, core = dp // 2, dp % 2
    col, row = me // n_y, me % n_y
    experts = n_x * n_y
    long, short = n_z // 2, n_z // 2 - 1
    sign = 1 - 2 * core
    other = z * 2 + 1 - core
    width = cotangent_ref.shape[1] // halves
    share = weights_ref.shape[0]

    def along_z(step):
        return lax.rem(z + step + 2 * n_z, n_z)

    def at_z(step):
        return along_z(step) * 2 + core

    def partner(offset):
        return lax.rem(col + offset // n_y, n_x) * n_y + lax.rem(row + offset % n_y, n_y)

    order = []
    for step in range(long):
        order.append((-(long - step), "away", step))
        if step < short:
            order.append((short - step, "toward", step))
    order.append((0, "own", 0))

    live_rows = lax.broadcasted_iota(jnp.int32, cotangent_ref.shape, 0) < count_ref[0]
    masked[...] = jnp.where(live_rows, cotangent_ref[...], jnp.zeros(cotangent_ref.shape, bf16))
    state[:, 0] = weights_ref[...].reshape(state.shape[0], 2, -1)
    state[:, 1] = first_ref[...].reshape(state.shape[0], 2, -1)
    state[:, 2] = second_ref[...].reshape(state.shape[0], 2, -1)

    barrier = pltpu.get_barrier_semaphore()
    pl.semaphore_signal(barrier, inc=1, device_id=(other, me), device_id_type=MESH)
    pl.semaphore_signal(barrier, inc=1, device_id=(at_z(1), me), device_id_type=MESH)
    pl.semaphore_signal(barrier, inc=1, device_id=(at_z(-1), me), device_id_type=MESH)

    @pl.loop(1, experts)
    def _(offset):
        pl.semaphore_signal(barrier, inc=1, device_id=(dp, partner(offset)), device_id_type=MESH)

    pl.semaphore_wait(barrier, experts + 2)

    def columns_of(step, parity):
        return pl.ds(pl.multiple_of((along_z(step) * 2 + parity) * share, share), share)

    pair = [
        pltpu.make_async_remote_copy(
            masked, masked_other, pair_send.at[len(order)], pair_recv.at[len(order)],
            device_id=(other, me), device_id_type=MESH,
        )
    ]
    for k, (step, _, _) in enumerate(order):
        pair.append(
            pltpu.make_async_remote_copy(
                inputs_ref.at[:, columns_of(-sign * step, 1 - core)], inputs_other.at[k],
                pair_send.at[k], pair_recv.at[k], device_id=(other, me), device_id_type=MESH,
            )
        )
    for copy in pair:
        copy.start()

    @pl.loop(1, experts)
    def _(offset):
        to = partner(offset)
        pltpu.make_async_remote_copy(
            state.at[to], state_all.at[me], state_send, state_recv, device_id=(dp, to), device_id_type=MESH
        ).start()

    own_state = pltpu.make_async_copy(state.at[me], state_all.at[me], own_sem.at[0])
    own_state.start()

    def product(k, half):
        cols = slice(half * width, (half + 1) * width)
        dims = (((0,), (0,)), ((), ()))
        mine = inputs_ref[:, columns_of(sign * order[k][0], core)]
        return lax.dot_general(mine, masked[:, cols], dims, preferred_element_type=f32) + lax.dot_general(
            inputs_other[k], masked_other[:, cols], dims, preferred_element_type=f32
        )

    def hop(buffers, sends, recvs, step, half, to):
        return pltpu.make_async_remote_copy(
            buffers.at[0, step, half], buffers.at[1, step, half], sends.at[step, half], recvs.at[step, half],
            device_id=(to, me), device_id_type=MESH,
        )

    hops = {"away": (away, away_send, away_recv, at_z(-sign)), "toward": (toward, toward_send, toward_recv, at_z(sign))}
    copies = {}
    pair[0].wait_recv()
    for k, (_, way, step) in enumerate(order):
        pair[k + 1].wait_recv()
        for half in range(halves):
            total = product(k, half)
            if way == "own":
                sources = [("away", long - 1)] + ([("toward", short - 1)] if short else [])
            else:
                sources = [(way, step - 1)] if step else []
            for name, before in sources:
                copies[name, before, half].wait_recv()
                total += hops[name][0][1, before, half].astype(f32)
            if way == "own":
                grad[:, :, half * width : (half + 1) * width] = total.astype(bf16).reshape(experts, 2, width)
            else:
                buffers, sends, recvs, to = hops[way]
                buffers[0, step, half] = total.astype(bf16)
                copies[way, step, half] = hop(buffers, sends, recvs, step, half, to)
                copies[way, step, half].start()

    @pl.loop(1, experts)
    def _(offset):
        to = partner(offset)
        pltpu.make_async_remote_copy(
            grad.at[to], grad_all.at[me], grad_send, grad_recv, device_id=(dp, to), device_id_type=MESH
        ).start()

    own_grad = pltpu.make_async_copy(grad.at[me], grad_all.at[me], own_sem.at[1])
    own_grad.start()

    def wait_all(ref, sem):
        part = ref.at[pl.ds(0, experts - 1)]
        pltpu.make_async_copy(part, part, sem).wait()

    own_state.wait()
    wait_all(state_all, state_recv)
    own_grad.wait()
    wait_all(grad_all, grad_recv)

    @pl.loop(0, experts, unroll=4)
    def _(e):
        new = adamw_step(
            grad_all[e].astype(f32),
            state_all[e, 0].astype(f32),
            state_all[e, 1].astype(f32),
            state_all[e, 2].astype(f32),
        )
        for a in range(3):
            updated[e, a] = new[a]

    def choose(to):
        picked = []
        for slot in range(2):
            source = table_ref[2 * to + slot]
            values = updated[jnp.maximum(source, 0)]
            picked.append(jnp.where(source >= 0, values, jnp.zeros_like(values)))
        for a in range(3):
            for r in range(2):
                pairs = [p[a, r : r + 1] for p in picked]
                chosen[to, a, r] = jnp.concatenate(pairs, axis=0).astype(bf16)

    mine = out_ref.at[:, pl.ds(me * 2, 2)]

    @pl.loop(1, experts)
    def _(offset):
        to = partner(offset)
        choose(to)
        pltpu.make_async_remote_copy(
            chosen.at[to], mine, out_send, out_recv, device_id=(dp, to), device_id_type=MESH
        ).start()

    choose(me)
    own_out = pltpu.make_async_copy(chosen.at[me], mine, own_sem.at[2])
    own_out.start()

    for copy in pair:
        copy.wait_send()
    for copy in copies.values():
        copy.wait_send()
    wait_all(state, state_send)
    wait_all(grad, grad_send)
    wait_all(chosen, out_send)
    own_out.wait()
    landed = out_ref.at[:, pl.ds(0, 2 * (experts - 1))]
    pltpu.make_async_copy(landed, landed, out_recv).wait()


def shards(
    n_dp, n_experts,
    expert_inputs, up_cotangent, row_counts, weights, first_moment, second_moment, old_expert, new_expert, slot_counts,
):
    inputs, cotangent = expert_inputs[0, 0], up_cotangent[0, 0]
    n_z = n_dp // 2
    n_x = n_y = math.isqrt(n_experts)
    rows, ff = cotangent.shape
    share = weights.shape[0]
    halves = 2
    long, short = n_z // 2, max(n_z // 2 - 1, 1)

    matches = old_expert[None, :] == new_expert[:, None]
    positions = jnp.arange(n_experts, dtype=jnp.int32)
    source = jnp.sum(jnp.where(matches, positions[None, :], 0), axis=1)
    keep = (jnp.arange(2, dtype=jnp.int32)[None, :] < slot_counts[:, None]).reshape(-1)
    table = jnp.where(keep, source, -1)

    vmem = pl.BlockSpec(memory_space=pltpu.VMEM)
    smem = pl.BlockSpec(memory_space=pltpu.SMEM)
    dma = pltpu.SemaphoreType.DMA
    out = pl.pallas_call(
        functools.partial(kernel, n_z, n_x, n_y, halves),
        out_shape=jax.ShapeDtypeStruct((3, share, 2, ff), bf16),
        in_specs=[smem, smem, vmem, vmem, vmem, vmem, vmem],
        out_specs=pl.BlockSpec(memory_space=pl.ANY),
        scratch_shapes=[
            pltpu.VMEM((rows, ff), bf16),
            pltpu.VMEM((rows, ff), bf16),
            pltpu.VMEM((n_z, rows, share), bf16),
            pltpu.VMEM((2, long, halves, share, ff // halves), bf16),
            pltpu.VMEM((2, short, halves, share, ff // halves), bf16),
            pltpu.VMEM((n_experts, 3, 2, ff), bf16),
            pltpu.VMEM((n_experts, 3, 2, ff), bf16),
            pltpu.VMEM((n_experts, 2, ff), bf16),
            pltpu.VMEM((n_experts, 2, ff), bf16),
            pltpu.VMEM((n_experts, 3, 2, ff), f32),
            pltpu.VMEM((n_experts, 3, 2, 2, ff), bf16),
            dma((n_z + 1,)), dma((n_z + 1,)),
            dma((long, halves)), dma((long, halves)),
            dma((short, halves)), dma((short, halves)),
            dma, dma, dma, dma, dma, dma,
            dma((3,)),
        ],
        compiler_params=pltpu.CompilerParams(collective_id=0, has_side_effects=True, vmem_limit_bytes=32 << 20),
        name="reduce_update_place",
    )(
        row_counts[0], table, inputs, cotangent,
        weights[:, 0], first_moment[:, 0], second_moment[:, 0],
    )
    return out[0], out[1], out[2]


def solution(mesh):
    return jax.shard_map(
        functools.partial(shards, mesh.shape["dp"], mesh.shape["expert"]),
        mesh=mesh,
        in_specs=(
            P("dp", "expert", None, None),
            P("dp", "expert", None, None),
            P("dp", "expert"),
            P("dp", "expert", None),
            P("dp", "expert", None),
            P("dp", "expert", None),
            P(),
            P(),
            P(),
        ),
        out_specs=(P("dp", "expert", None), P("dp", "expert", None), P("dp", "expert", None)),
        check_vma=False,
    )
```

```python
import functools
import math

import jax
import jax.numpy as jnp
from jax import lax
from jax.experimental import pallas as pl
from jax.experimental.pallas import tpu as pltpu
from jax.sharding import PartitionSpec as P

MESH = pl.DeviceIdType.MESH
f32, bf16 = jnp.float32, jnp.bfloat16

beta_one = 0.9
beta_two = 0.95
learn_rate = 0.05
decay_rate = 0.1
epsilon = 1e-08
correct_one = 0.9999734386011124
correct_two = 0.994079470779666


def adamw_step(gradient, weight, first, second):
    first_new = beta_one * first + (1.0 - beta_one) * gradient
    second_new = beta_two * second + (1.0 - beta_two) * gradient * gradient
    scaled = second_new * (1.0 / correct_two)
    root = scaled * lax.rsqrt(scaled)
    weight_new = (1.0 - learn_rate * decay_rate) * weight - (learn_rate / correct_one) * first_new / (root + epsilon)
    return weight_new, first_new, second_new


def kernel(
    n_z, n_x, n_y, widths, lag,
    count_ref, old_ref, live_ref, new_ref, inputs_ref, cotangent_ref, weights_ref, first_ref, second_ref,
    out_ref,
    inputs, cotangent, moments, names, places, table,
    masked, masked_other, inputs_other, away, toward, state, state_all, grad, grad_all, updated, chosen, relay,
    load_sem, pair_send, pair_recv, away_send, away_recv, toward_send, toward_recv,
    state_send, state_recv, grad_send, grad_recv, out_send, out_recv, own_sem, relay_send, relay_recv,
):
    dp, me = lax.axis_index("dp"), lax.axis_index("expert")
    z, core = dp // 2, dp % 2
    col, row = me // n_y, me % n_y
    experts = n_x * n_y
    long, short = n_z // 2, n_z // 2 - 1
    sign = 1 - 2 * core
    other = z * 2 + 1 - core
    parts = len(widths)
    starts = [sum(widths[:part]) for part in range(parts)]
    share = weights_ref.shape[0]

    def along_z(step):
        return lax.rem(z + step + 2 * n_z, n_z)

    def at_z(step):
        return along_z(step) * 2 + core

    def at(dx, dy):
        return lax.rem(col + dx + n_x, n_x) * n_y + lax.rem(row + dy + n_y, n_y)

    def steps_of(offset):
        offset = lax.rem(offset * 27, experts)
        return offset // n_y, offset % n_y

    def partner(offset):
        return at(*steps_of(offset))

    half_x, half_y = n_x // 2, n_y // 2

    def is_direct(offset):
        dx, dy = steps_of(offset)
        return jnp.logical_not(RELAY & (((dx == half_x) & (dy < half_y)) | ((dy == half_y) & (dx < half_x))))

    def relays():
        for j in range(half_y):
            yield 0, j, at(half_x, j), at(-(half_x // 2), 0), at(-(half_x // 2), j), at(half_x // 2, 0)
        for j in range(half_x):
            yield 1, j, at(j, half_y), at(0, -(half_y // 2)), at(j, -(half_y // 2)), at(0, half_y // 2)

    def used(ref, part):
        here = ref.at[part]
        return here.at[(slice(None),) * (len(here.shape) - 1) + (pl.ds(0, widths[part]),)]

    barrier = pltpu.get_barrier_semaphore()
    pl.semaphore_signal(barrier, inc=1, device_id=(other, me), device_id_type=MESH)
    pl.semaphore_signal(barrier, inc=1, device_id=(at_z(1), me), device_id_type=MESH)
    pl.semaphore_signal(barrier, inc=1, device_id=(at_z(-1), me), device_id_type=MESH)

    @pl.loop(1, experts)
    def _(offset):
        pl.semaphore_signal(barrier, inc=1, device_id=(dp, partner(offset)), device_id_type=MESH)

    loads = [
        pltpu.make_async_copy(source, target, load_sem.at[i])
        for i, (source, target) in enumerate(
            [
                (cotangent_ref, cotangent),
                (inputs_ref, inputs),
                (new_ref, names),
                (weights_ref, moments.at[0]),
                (first_ref, moments.at[1]),
                (second_ref, moments.at[2]),
            ]
        )
    ]
    for copy in loads:
        copy.start()

    order = []
    for step in range(long):
        order.append((-(long - step), "away", step))
        if step < short:
            order.append((short - step, "toward", step))
    order.append((0, "own", 0))

    loads[0].wait()
    live_rows = lax.broadcasted_iota(jnp.int32, cotangent.shape, 0) < count_ref[0]
    masked[...] = jnp.where(live_rows, cotangent[...], jnp.zeros(cotangent.shape, bf16))
    loads[1].wait()
    pl.semaphore_wait(barrier, experts + 2)

    def columns_of(step, parity):
        return pl.ds(pl.multiple_of((along_z(step) * 2 + parity) * share, share), share)

    masks = []
    for part in range(parts):
        cols = slice(starts[part], starts[part] + widths[part])
        masks.append(
            pltpu.make_async_remote_copy(
                masked.at[:, cols], masked_other.at[:, cols],
                pair_send.at[len(order) + part], pair_recv.at[len(order) + part],
                device_id=(other, me), device_id_type=MESH,
            )
        )
    pair = list(masks)
    for k, (step, _, _) in enumerate(order):
        pair.append(
            pltpu.make_async_remote_copy(
                inputs.at[:, columns_of(-sign * step, 1 - core)], inputs_other.at[k],
                pair_send.at[k], pair_recv.at[k], device_id=(other, me), device_id_type=MESH,
            )
        )
    starting = [pair[0], pair[parts], pair[parts + 1], *pair[1:parts], *pair[parts + 2 :]]
    for copy in starting:
        copy.start()

    loads[2].wait()
    slots = lax.broadcasted_iota(jnp.int32, names.shape, 1)

    def place(e, carry):
        found, dead = carry
        found = jnp.where(names[...] == old_ref[e], e, found)
        dead = jnp.where((slots >= 2 * e + live_ref[e]) & (slots < 2 * e + 2), 1, dead)
        return found, dead

    zeros = jnp.zeros(names.shape, jnp.int32)
    found, dead = lax.fori_loop(0, experts, place, (zeros, zeros))
    places[...] = jnp.where(dead == 1, -1, found)
    to_scalars = pltpu.make_async_copy(places, table, load_sem.at[6])
    to_scalars.start()

    for a in range(3):
        loads[3 + a].wait()
        state[:, a] = moments[a].reshape(experts, 2, -1)

    def send_state(first, last):
        @pl.loop(first, last)
        def _(offset):
            to = partner(offset)
            pltpu.make_async_remote_copy(
                state.at[to], state_all.at[me], state_send, state_recv, device_id=(dp, to), device_id_type=MESH
            ).start()

    own_state = pltpu.make_async_copy(state.at[me], state_all.at[me], own_sem.at[2 * parts])
    own_state.start()

    def product(k, part):
        cols = slice(starts[part], starts[part] + widths[part])
        dims = (((0,), (0,)), ((), ()))
        mine = inputs[:, columns_of(sign * order[k][0], core)]
        return lax.dot_general(mine, masked[:, cols], dims, preferred_element_type=f32) + lax.dot_general(
            inputs_other[k], masked_other[:, cols], dims, preferred_element_type=f32
        )

    hops = {"away": (away, away_send, away_recv, at_z(-sign)), "toward": (toward, toward_send, toward_recv, at_z(sign))}
    copies = {}

    def reduce(k, part):
        _, way, step = order[k]
        total = product(k, part)
        if way == "own":
            sources = [("away", long - 1)] + ([("toward", short - 1)] if short else [])
        else:
            sources = [(way, step - 1)] if step else []
        for name, before in sources:
            copies[name, before, part].wait_recv()
            total += hops[name][0][1, before, part, :, : widths[part]].astype(f32)
        if way == "own":
            grad[part, :, :, : widths[part]] = total.astype(bf16).reshape(experts, 2, widths[part])
            send_grad(part)
        else:
            buffers, sends, recvs, to = hops[way]
            buffers[0, step, part, :, : widths[part]] = total.astype(bf16)
            copies[way, step, part] = pltpu.make_async_remote_copy(
                buffers.at[0, step, part, :, pl.ds(0, widths[part])], buffers.at[1, step, part, :, pl.ds(0, widths[part])],
                sends.at[step, part], recvs.at[step, part],
                device_id=(to, me), device_id_type=MESH,
            )
            copies[way, step, part].start()

    own_copies = []

    def send_grad(part):
        @pl.loop(1, experts)
        def _(offset):
            to = partner(offset)
            pltpu.make_async_remote_copy(
                used(grad, part).at[to], used(grad_all, part).at[me], grad_send.at[part], grad_recv.at[part],
                device_id=(dp, to), device_id_type=MESH,
            ).start()

        own_copies.append(
            pltpu.make_async_copy(used(grad, part).at[me], used(grad_all, part).at[me], own_sem.at[part])
        )
        own_copies[-1].start()

    def wait_all(ref, sem):
        part = ref.at[pl.ds(0, experts - 1)]
        pltpu.make_async_copy(part, part, sem).wait()

    def update(part):
        cols = slice(starts[part], starts[part] + widths[part])
        if part == 0:
            own_state.wait()
            wait_all(state_all, state_recv)
        own_copies[part].wait()
        wait_all(used(grad_all, part), grad_recv.at[part])

        batch = min(8, experts)

        @pl.loop(0, experts // batch)
        def _(i):
            some = pl.ds(i * batch, batch)
            new = adamw_step(
                grad_all[part, some, :, : widths[part]].astype(f32),
                state_all[some, 0, :, cols].astype(f32),
                state_all[some, 1, :, cols].astype(f32),
                state_all[some, 2, :, cols].astype(f32),
            )
            for a in range(3):
                updated[part, some, a, :, : widths[part]] = new[a]

    def choose(part, to):
        picked = []
        for slot in range(2):
            source = table[0, 2 * to + slot]
            values = updated[part, jnp.maximum(source, 0), :, :, : widths[part]]
            picked.append(jnp.where(source >= 0, values, jnp.zeros_like(values)))
        for a in range(3):
            for r in range(2):
                pairs = [p[a, r : r + 1] for p in picked]
                chosen[part, to, a, r, :, : widths[part]] = jnp.concatenate(pairs, axis=0).astype(bf16)

    def landing(part, source=me):
        return out_ref.at[:, pl.ds(source * 2, 2), :, pl.ds(starts[part], widths[part])]

    def relay_chosen(part):
        for axis, j, to, by, _, _ in relays():
            choose(part, to)
            pltpu.make_async_remote_copy(
                used(chosen, part).at[to], used(relay, part).at[axis, j], relay_send.at[part], relay_recv.at[part],
                device_id=(dp, by), device_id_type=MESH,
            ).start()

    def forward_chosen(part):
        here = used(relay, part)
        pltpu.make_async_copy(here, here, relay_recv.at[part]).wait()
        for axis, j, _, _, to, source in relays():
            pltpu.make_async_remote_copy(
                here.at[axis, j], landing(part, source), relay_send.at[part], out_recv.at[part],
                device_id=(dp, to), device_id_type=MESH,
            ).start()

    def send_chosen(part, first, last):
        @pl.loop(first, last)
        def _(offset):
            to = partner(offset)

            @pl.when(is_direct(offset))
            def _():
                choose(part, to)
                pltpu.make_async_remote_copy(
                    used(chosen, part).at[to], landing(part), out_send.at[part], out_recv.at[part],
                    device_id=(dp, to), device_id_type=MESH,
                ).start()

        if last == experts:
            choose(part, me)
            own_copies.append(
                pltpu.make_async_copy(used(chosen, part).at[me], landing(part), own_sem.at[parts + part])
            )
            own_copies[-1].start()

    steps = sorted((k + lag * part, part, k) for part in range(parts) for k in range(len(order)))
    spread = 1
    middle = 1 + experts // EARLY

    def finish(part):
        if part == 0:
            to_scalars.wait()
        update(part)
        if RELAY:
            relay_chosen(part)
        send_chosen(part, 1, middle)

    def finish_rest(part):
        send_chosen(part, middle, experts)
        if RELAY:
            forward_chosen(part)

    for i, (_, part, k) in enumerate(steps):
        if part == 0:
            pair[k + parts].wait_recv()
        if k == 0:
            masks[part].wait_recv()
        if order[k][1] == "own" and part > 0:
            finish(part - 1)
        reduce(k, part)
        if order[k][1] == "own" and part > 0:
            finish_rest(part - 1)
        until = 1 + (experts - 1) * min(i + 1, len(order)) // len(order)
        if until > spread:
            send_state(spread, until)
            spread = until
    finish(parts - 1)
    finish_rest(parts - 1)

    for copy in pair:
        copy.wait_send()
    for copy in copies.values():
        copy.wait_send()
    wait_all(state, state_send)
    direct = experts - 1 - (half_x + half_y if RELAY else 0)
    for part in range(parts):
        wait_all(used(grad, part), grad_send.at[part])
        sent = used(chosen, part).at[pl.ds(0, direct)]
        pltpu.make_async_copy(sent, sent, out_send.at[part]).wait()
        if RELAY:
            here = used(relay, part)
            for _ in range(2):
                pltpu.make_async_copy(here, here, relay_send.at[part]).wait()
        own_copies[parts + part].wait()
        landed = out_ref.at[:, pl.ds(0, 2 * (experts - 1)), :, pl.ds(starts[part], widths[part])]
        pltpu.make_async_copy(landed, landed, out_recv.at[part]).wait()


RELAY = False
SPLIT, LAG, EARLY = (1, 2), 2, 4


def shards(
    n_dp, n_experts,
    expert_inputs, up_cotangent, row_counts, weights, first_moment, second_moment, old_expert, new_expert, slot_counts,
):
    inputs, cotangent = expert_inputs[0, 0], up_cotangent[0, 0]
    n_z = n_dp // 2
    n_x = n_y = math.isqrt(n_experts)
    rows, ff = cotangent.shape
    share = weights.shape[0]
    long, short = n_z // 2, max(n_z // 2 - 1, 1)
    widths = [ff * w // sum(SPLIT) for w in SPLIT]
    parts, width = len(widths), max(widths)

    hbm = pl.BlockSpec(memory_space=pltpu.HBM)
    smem = pl.BlockSpec(memory_space=pltpu.SMEM)
    dma = pltpu.SemaphoreType.DMA
    out = pl.pallas_call(
        functools.partial(kernel, n_z, n_x, n_y, widths, LAG),
        out_shape=jax.ShapeDtypeStruct((3, share, 2, ff), bf16),
        in_specs=[smem] * 3 + [hbm] * 6,
        out_specs=hbm,
        scratch_shapes=[
            pltpu.VMEM(inputs.shape, bf16),
            pltpu.VMEM((rows, ff), bf16),
            pltpu.VMEM((3, share, ff), bf16),
            pltpu.VMEM((1, 2 * n_experts), jnp.int32),
            pltpu.VMEM((1, 2 * n_experts), jnp.int32),
            pltpu.SMEM((1, 2 * n_experts), jnp.int32),
            pltpu.VMEM((rows, ff), bf16),
            pltpu.VMEM((rows, ff), bf16),
            pltpu.VMEM((n_z, rows, share), bf16),
            pltpu.VMEM((2, long, parts, share, width), bf16),
            pltpu.VMEM((2, short, parts, share, width), bf16),
            pltpu.VMEM((n_experts, 3, 2, ff), bf16),
            pltpu.VMEM((n_experts, 3, 2, ff), bf16),
            pltpu.VMEM((parts, n_experts, 2, width), bf16),
            pltpu.VMEM((parts, n_experts, 2, width), bf16),
            pltpu.VMEM((parts, n_experts, 3, 2, width), f32),
            pltpu.VMEM((parts, n_experts, 3, 2, 2, width), bf16),
            pltpu.VMEM((parts, 2, n_x // 2, 3, 2, 2, width), bf16),
            dma((7,)),
            dma((n_z + parts,)), dma((n_z + parts,)),
            dma((long, parts)), dma((long, parts)),
            dma((short, parts)), dma((short, parts)),
            dma, dma,
            dma((parts,)), dma((parts,)), dma((parts,)), dma((parts,)),
            dma((2 * parts + 1,)),
            dma((parts,)), dma((parts,)),
        ],
        compiler_params=pltpu.CompilerParams(collective_id=0, has_side_effects=True, vmem_limit_bytes=56 << 20),
        name="reduce_update_place",
    )(
        row_counts[0], old_expert, slot_counts, new_expert[None], inputs, cotangent,
        weights[:, 0], first_moment[:, 0], second_moment[:, 0],
    )
    return out[0], out[1], out[2]


def solution(mesh):
    return jax.shard_map(
        functools.partial(shards, mesh.shape["dp"], mesh.shape["expert"]),
        mesh=mesh,
        in_specs=(
            P("dp", "expert", None, None),
            P("dp", "expert", None, None),
            P("dp", "expert"),
            P("dp", "expert", None),
            P("dp", "expert", None),
            P("dp", "expert", None),
            P(),
            P(),
            P(),
        ),
        out_specs=(P("dp", "expert", None), P("dp", "expert", None), P("dp", "expert", None)),
        check_vma=False,
    )
```

```python
import functools
import math

import jax
import jax.numpy as jnp
from jax import lax
from jax.experimental import pallas as pl
from jax.experimental.pallas import tpu as pltpu
from jax.sharding import PartitionSpec as P

MESH = pl.DeviceIdType.MESH
f32, bf16 = jnp.float32, jnp.bfloat16

beta_one = 0.9
beta_two = 0.95
learn_rate = 0.05
decay_rate = 0.1
epsilon = 1e-08
correct_one = 0.9999734386011124
correct_two = 0.994079470779666


def adamw_step(gradient, weight, first, second):
    first_new = beta_one * first + (1.0 - beta_one) * gradient
    second_new = beta_two * second + (1.0 - beta_two) * gradient * gradient
    scaled = second_new * (1.0 / correct_two)
    root = scaled * lax.rsqrt(scaled)
    weight_new = (1.0 - learn_rate * decay_rate) * weight - (learn_rate / correct_one) * first_new / (root + epsilon)
    return weight_new, first_new, second_new


def kernel(
    n_z, n_x, n_y, widths, lag,
    count_ref, old_ref, live_ref, new_ref, inputs_ref, cotangent_ref, weights_ref, first_ref, second_ref,
    out_ref,
    inputs, cotangent, moments, names, places, table,
    masked, masked_other, inputs_other, own_terms, away, toward, state, state_all, grad, grad_all, updated, chosen, relay,
    load_sem, pair_send, pair_recv, away_send, away_recv, toward_send, toward_recv,
    state_send, state_recv, grad_send, grad_recv, out_send, out_recv, own_sem, relay_send, relay_recv,
):
    dp, me = lax.axis_index("dp"), lax.axis_index("expert")
    z, core = dp // 2, dp % 2
    col, row = me // n_y, me % n_y
    experts = n_x * n_y
    long, short = n_z // 2, n_z // 2 - 1
    sign = 1 - 2 * core
    other = z * 2 + 1 - core
    parts = len(widths)
    starts = [sum(widths[:part]) for part in range(parts)]
    share = weights_ref.shape[0]

    def along_z(step):
        return lax.rem(z + step + 2 * n_z, n_z)

    def at_z(step):
        return along_z(step) * 2 + core

    def at(dx, dy):
        return lax.rem(col + dx + n_x, n_x) * n_y + lax.rem(row + dy + n_y, n_y)

    def steps_of(offset):
        offset = lax.rem(offset * 27, experts)
        return offset // n_y, offset % n_y

    def partner(offset):
        return at(*steps_of(offset))

    half_x, half_y = n_x // 2, n_y // 2

    def is_direct(offset):
        dx, dy = steps_of(offset)
        return jnp.logical_not(RELAY & (((dx == half_x) & (dy < half_y)) | ((dy == half_y) & (dx < half_x))))

    def relays():
        for j in range(half_y):
            yield 0, j, at(half_x, j), at(-(half_x // 2), 0), at(-(half_x // 2), j), at(half_x // 2, 0)
        for j in range(half_x):
            yield 1, j, at(j, half_y), at(0, -(half_y // 2)), at(j, -(half_y // 2)), at(0, half_y // 2)

    def used(ref, part):
        here = ref.at[part]
        return here.at[(slice(None),) * (len(here.shape) - 1) + (pl.ds(0, widths[part]),)]

    barrier = pltpu.get_barrier_semaphore()
    pl.semaphore_signal(barrier, inc=1, device_id=(other, me), device_id_type=MESH)
    pl.semaphore_signal(barrier, inc=1, device_id=(at_z(1), me), device_id_type=MESH)
    pl.semaphore_signal(barrier, inc=1, device_id=(at_z(-1), me), device_id_type=MESH)

    @pl.loop(1, experts)
    def _(offset):
        pl.semaphore_signal(barrier, inc=1, device_id=(dp, partner(offset)), device_id_type=MESH)

    loads = [
        pltpu.make_async_copy(source, target, load_sem.at[i])
        for i, (source, target) in enumerate(
            [
                (cotangent_ref, cotangent),
                (inputs_ref, inputs),
                (new_ref, names),
                (weights_ref, moments.at[0]),
                (first_ref, moments.at[1]),
                (second_ref, moments.at[2]),
            ]
        )
    ]
    for copy in loads:
        copy.start()

    order = []
    for step in range(long):
        order.append((-(long - step), "away", step))
        if step < short:
            order.append((short - step, "toward", step))
    order.append((0, "own", 0))

    loads[0].wait()
    live_rows = lax.broadcasted_iota(jnp.int32, cotangent.shape, 0) < count_ref[0]
    masked[...] = jnp.where(live_rows, cotangent[...], jnp.zeros(cotangent.shape, bf16))
    loads[1].wait()

    def columns_of(step, parity):
        return pl.ds(pl.multiple_of((along_z(step) * 2 + parity) * share, share), share)

    dims = (((0,), (0,)), ((), ()))
    for k, (step, _, _) in enumerate(order):
        mine = inputs[:, columns_of(sign * step, core)]
        own_terms[k] = lax.dot_general(mine, masked[...], dims, preferred_element_type=f32)
    pl.semaphore_wait(barrier, experts + 2)


    masks = []
    for part in range(parts):
        cols = slice(starts[part], starts[part] + widths[part])
        masks.append(
            pltpu.make_async_remote_copy(
                masked.at[:, cols], masked_other.at[:, cols],
                pair_send.at[len(order) + part], pair_recv.at[len(order) + part],
                device_id=(other, me), device_id_type=MESH,
            )
        )
    pair = list(masks)
    for k, (step, _, _) in enumerate(order):
        pair.append(
            pltpu.make_async_remote_copy(
                inputs.at[:, columns_of(-sign * step, 1 - core)], inputs_other.at[k],
                pair_send.at[k], pair_recv.at[k], device_id=(other, me), device_id_type=MESH,
            )
        )
    starting = [pair[0], pair[parts], pair[parts + 1], *pair[1:parts], *pair[parts + 2 :]]
    for copy in starting:
        copy.start()

    loads[2].wait()
    slots = lax.broadcasted_iota(jnp.int32, names.shape, 1)

    def place(e, carry):
        found, dead = carry
        found = jnp.where(names[...] == old_ref[e], e, found)
        dead = jnp.where((slots >= 2 * e + live_ref[e]) & (slots < 2 * e + 2), 1, dead)
        return found, dead

    zeros = jnp.zeros(names.shape, jnp.int32)
    found, dead = lax.fori_loop(0, experts, place, (zeros, zeros))
    places[...] = jnp.where(dead == 1, -1, found)
    to_scalars = pltpu.make_async_copy(places, table, load_sem.at[6])
    to_scalars.start()

    for a in range(3):
        loads[3 + a].wait()
        state[:, a] = moments[a].reshape(experts, 2, -1)

    def send_state(first, last):
        @pl.loop(first, last)
        def _(offset):
            to = partner(offset)
            pltpu.make_async_remote_copy(
                state.at[to], state_all.at[me], state_send, state_recv, device_id=(dp, to), device_id_type=MESH
            ).start()

    own_state = pltpu.make_async_copy(state.at[me], state_all.at[me], own_sem.at[2 * parts])
    own_state.start()

    def product(k, part):
        cols = slice(starts[part], starts[part] + widths[part])
        return own_terms[k, :, cols] + lax.dot_general(
            inputs_other[k], masked_other[:, cols], dims, preferred_element_type=f32
        )

    hops = {"away": (away, away_send, away_recv, at_z(-sign)), "toward": (toward, toward_send, toward_recv, at_z(sign))}
    copies = {}

    def reduce(k, part):
        _, way, step = order[k]
        total = product(k, part)
        if way == "own":
            sources = [("away", long - 1)] + ([("toward", short - 1)] if short else [])
        else:
            sources = [(way, step - 1)] if step else []
        for name, before in sources:
            copies[name, before, part].wait_recv()
            total += hops[name][0][1, before, part, :, : widths[part]].astype(f32)
        if way == "own":
            grad[part, :, :, : widths[part]] = total.astype(bf16).reshape(experts, 2, widths[part])
            send_grad(part)
        else:
            buffers, sends, recvs, to = hops[way]
            buffers[0, step, part, :, : widths[part]] = total.astype(bf16)
            copies[way, step, part] = pltpu.make_async_remote_copy(
                buffers.at[0, step, part, :, pl.ds(0, widths[part])], buffers.at[1, step, part, :, pl.ds(0, widths[part])],
                sends.at[step, part], recvs.at[step, part],
                device_id=(to, me), device_id_type=MESH,
            )
            copies[way, step, part].start()

    own_copies = []

    def send_grad(part):
        @pl.loop(1, experts)
        def _(offset):
            to = partner(offset)
            pltpu.make_async_remote_copy(
                used(grad, part).at[to], used(grad_all, part).at[me], grad_send.at[part], grad_recv.at[part],
                device_id=(dp, to), device_id_type=MESH,
            ).start()

        own_copies.append(
            pltpu.make_async_copy(used(grad, part).at[me], used(grad_all, part).at[me], own_sem.at[part])
        )
        own_copies[-1].start()

    def wait_all(ref, sem):
        part = ref.at[pl.ds(0, experts - 1)]
        pltpu.make_async_copy(part, part, sem).wait()

    def update(part):
        cols = slice(starts[part], starts[part] + widths[part])
        if part == 0:
            own_state.wait()
            wait_all(state_all, state_recv)
        own_copies[part].wait()
        wait_all(used(grad_all, part), grad_recv.at[part])

        batch = min(8, experts)

        @pl.loop(0, experts // batch)
        def _(i):
            some = pl.ds(i * batch, batch)
            new = adamw_step(
                grad_all[part, some, :, : widths[part]].astype(f32),
                state_all[some, 0, :, cols].astype(f32),
                state_all[some, 1, :, cols].astype(f32),
                state_all[some, 2, :, cols].astype(f32),
            )
            for a in range(3):
                updated[part, some, a, :, : widths[part]] = new[a]

    def choose(part, to):
        picked = []
        for slot in range(2):
            source = table[0, 2 * to + slot]
            values = updated[part, jnp.maximum(source, 0), :, :, : widths[part]]
            picked.append(jnp.where(source >= 0, values, jnp.zeros_like(values)))
        for a in range(3):
            for r in range(2):
                pairs = [p[a, r : r + 1] for p in picked]
                chosen[part, to, a, r, :, : widths[part]] = jnp.concatenate(pairs, axis=0).astype(bf16)

    def landing(part, source=me):
        return out_ref.at[:, pl.ds(source * 2, 2), :, pl.ds(starts[part], widths[part])]

    def relay_chosen(part):
        for axis, j, to, by, _, _ in relays():
            choose(part, to)
            pltpu.make_async_remote_copy(
                used(chosen, part).at[to], used(relay, part).at[axis, j], relay_send.at[part], relay_recv.at[part],
                device_id=(dp, by), device_id_type=MESH,
            ).start()

    def forward_chosen(part):
        here = used(relay, part)
        pltpu.make_async_copy(here, here, relay_recv.at[part]).wait()
        for axis, j, _, _, to, source in relays():
            pltpu.make_async_remote_copy(
                here.at[axis, j], landing(part, source), relay_send.at[part], out_recv.at[part],
                device_id=(dp, to), device_id_type=MESH,
            ).start()

    def send_chosen(part, first, last):
        @pl.loop(first, last)
        def _(offset):
            to = partner(offset)

            @pl.when(is_direct(offset))
            def _():
                choose(part, to)
                pltpu.make_async_remote_copy(
                    used(chosen, part).at[to], landing(part), out_send.at[part], out_recv.at[part],
                    device_id=(dp, to), device_id_type=MESH,
                ).start()

        if last == experts:
            choose(part, me)
            own_copies.append(
                pltpu.make_async_copy(used(chosen, part).at[me], landing(part), own_sem.at[parts + part])
            )
            own_copies[-1].start()

    steps = sorted((k + lag * part, part, k) for part in range(parts) for k in range(len(order)))
    spread = 1
    middle = 1 + experts // EARLY

    def finish(part):
        if part == 0:
            to_scalars.wait()
        update(part)
        if RELAY:
            relay_chosen(part)
        send_chosen(part, 1, middle)

    def finish_rest(part):
        send_chosen(part, middle, experts)
        if RELAY:
            forward_chosen(part)

    for i, (_, part, k) in enumerate(steps):
        if part == 0:
            pair[k + parts].wait_recv()
        if k == 0:
            masks[part].wait_recv()
        if order[k][1] == "own" and part > 0:
            finish(part - 1)
        reduce(k, part)
        if order[k][1] == "own" and part > 0:
            finish_rest(part - 1)
        until = 1 + (experts - 1) * min(i + 1, len(order)) // len(order)
        if until > spread:
            send_state(spread, until)
            spread = until
    finish(parts - 1)
    finish_rest(parts - 1)

    for copy in pair:
        copy.wait_send()
    for copy in copies.values():
        copy.wait_send()
    wait_all(state, state_send)
    direct = experts - 1 - (half_x + half_y if RELAY else 0)
    for part in range(parts):
        wait_all(used(grad, part), grad_send.at[part])
        sent = used(chosen, part).at[pl.ds(0, direct)]
        pltpu.make_async_copy(sent, sent, out_send.at[part]).wait()
        if RELAY:
            here = used(relay, part)
            for _ in range(2):
                pltpu.make_async_copy(here, here, relay_send.at[part]).wait()
        own_copies[parts + part].wait()
        landed = out_ref.at[:, pl.ds(0, 2 * (experts - 1)), :, pl.ds(starts[part], widths[part])]
        pltpu.make_async_copy(landed, landed, out_recv.at[part]).wait()


def split(all_ref, weights_ref, first_ref, second_ref, held, load_sem, store_sem):
    size = all_ref.shape[1] // 2
    loads, stores = [], []
    for i in range(2):
        rows = pl.ds(i * size, size)
        for a, ref in enumerate([weights_ref, first_ref, second_ref]):
            loads.append(pltpu.make_async_copy(all_ref.at[a, rows], held.at[a, rows], load_sem.at[a, i]))
            stores.append(pltpu.make_async_copy(held.at[a, rows], ref.at[rows], store_sem.at[a, i]))
    for copy in loads:
        copy.start()
    for load, store in zip(loads, stores):
        load.wait()
        store.start()
    for copy in stores:
        copy.wait()


RELAY = False
SPLIT, LAG, EARLY = (1, 2), 2, 4


def shards(
    n_dp, n_experts,
    expert_inputs, up_cotangent, row_counts, weights, first_moment, second_moment, old_expert, new_expert, slot_counts,
):
    inputs, cotangent = expert_inputs[0, 0], up_cotangent[0, 0]
    n_z = n_dp // 2
    n_x = n_y = math.isqrt(n_experts)
    rows, ff = cotangent.shape
    share = weights.shape[0]
    long, short = n_z // 2, max(n_z // 2 - 1, 1)
    widths = [ff * w // sum(SPLIT) for w in SPLIT]
    parts, width = len(widths), max(widths)

    hbm = pl.BlockSpec(memory_space=pltpu.HBM)
    smem = pl.BlockSpec(memory_space=pltpu.SMEM)
    dma = pltpu.SemaphoreType.DMA
    out = pl.pallas_call(
        functools.partial(kernel, n_z, n_x, n_y, widths, LAG),
        out_shape=jax.ShapeDtypeStruct((3, share, 2, ff), bf16),
        in_specs=[smem] * 3 + [hbm] * 6,
        out_specs=hbm,
        scratch_shapes=[
            pltpu.VMEM(inputs.shape, bf16),
            pltpu.VMEM((rows, ff), bf16),
            pltpu.VMEM((3, share, ff), bf16),
            pltpu.VMEM((1, 2 * n_experts), jnp.int32),
            pltpu.VMEM((1, 2 * n_experts), jnp.int32),
            pltpu.SMEM((1, 2 * n_experts), jnp.int32),
            pltpu.VMEM((rows, ff), bf16),
            pltpu.VMEM((rows, ff), bf16),
            pltpu.VMEM((n_z, rows, share), bf16),
            pltpu.VMEM((n_z, share, ff), f32),
            pltpu.VMEM((2, long, parts, share, width), bf16),
            pltpu.VMEM((2, short, parts, share, width), bf16),
            pltpu.VMEM((n_experts, 3, 2, ff), bf16),
            pltpu.VMEM((n_experts, 3, 2, ff), bf16),
            pltpu.VMEM((parts, n_experts, 2, width), bf16),
            pltpu.VMEM((parts, n_experts, 2, width), bf16),
            pltpu.VMEM((parts, n_experts, 3, 2, width), f32),
            pltpu.VMEM((parts, n_experts, 3, 2, 2, width), bf16),
            pltpu.VMEM((parts, 2, n_x // 2, 3, 2, 2, width), bf16),
            dma((7,)),
            dma((n_z + parts,)), dma((n_z + parts,)),
            dma((long, parts)), dma((long, parts)),
            dma((short, parts)), dma((short, parts)),
            dma, dma,
            dma((parts,)), dma((parts,)), dma((parts,)), dma((parts,)),
            dma((2 * parts + 1,)),
            dma((parts,)), dma((parts,)),
        ],
        compiler_params=pltpu.CompilerParams(collective_id=0, has_side_effects=True, vmem_limit_bytes=56 << 20),
        name="reduce_update_place",
    )(
        row_counts[0], old_expert, slot_counts, new_expert[None], inputs, cotangent,
        weights[:, 0], first_moment[:, 0], second_moment[:, 0],
    )
    each = jax.ShapeDtypeStruct((share, 2, ff), bf16)
    return pl.pallas_call(
        split,
        out_shape=(each, each, each),
        in_specs=[hbm],
        out_specs=(hbm, hbm, hbm),
        scratch_shapes=[pltpu.VMEM((3, share, 2, ff), bf16), dma((3, 2)), dma((3, 2))],
        compiler_params=pltpu.CompilerParams(vmem_limit_bytes=56 << 20),
        name="split_outputs",
    )(out)


def solution(mesh):
    return jax.shard_map(
        functools.partial(shards, mesh.shape["dp"], mesh.shape["expert"]),
        mesh=mesh,
        in_specs=(
            P("dp", "expert", None, None),
            P("dp", "expert", None, None),
            P("dp", "expert"),
            P("dp", "expert", None),
            P("dp", "expert", None),
            P("dp", "expert", None),
            P(),
            P(),
            P(),
        ),
        out_specs=(P("dp", "expert", None), P("dp", "expert", None), P("dp", "expert", None)),
        check_vma=False,
    )
```
